32 devices in a mesh: frame: 4 (over y, core), module: 8 (over z, x).
Axes of the slice: x: 2, y: 2, z: 4, core: 2. Of those that a mesh axis runs over, the one named last changes fastest.
Arguments:
- frames: bfloat16 [1024, 98304], P('frame', 'module'), may hold values from -6 to 6
- weights: bfloat16 [768, 512, 128], P('module'), may hold values from 0 to 0.25
- monitor: float32 [1024], P('frame'), may hold values from 0.5 to 2
- coverage: int32 [8, 96], replicated, may hold values from 0 to 255, as said below
- block_slot: int32 [8, 96], P('module'), may hold values from 0 to 95, each once within a row
- angle_index: int32 [2], replicated, may hold values from 0 to 179
Outputs:
- slices: bfloat16 [8, 4, 8, 128, 8192], P(None, 'frame', 'module')
The draws below stay inside these ranges and needn't reach their ends.
Inputs may be any that keep to these rules, and one draw needn't show every extreme that they name: `coverage`: row m holds 96 consecutive tile numbers s, s + 1, ... taken modulo 256, in order, for a start s of its own. `block_slot`: each row is a permutation.
All inputs are finite; a program needn't handle non-finite values.
Results may differ from the reference program's by a relative error of at most 0.0055.
Values sent between devices are 32-bit elements; how exact they have to be, the bound alone decides.
A program may use at most 192 MiB of HBM per device.

```python
import math
import jax
import jax.numpy as jnp
from jax import lax

TILE = 128
TRANS = 512
TPM = 96
SPLITS = 4
PB = 512
ASTEPS = 180
ROWS = 16
NTILE = 256
PIX = 12288
MODULES = 8
GROUPS = 4
FRAMES = 1024
ANGLES = 2
QT = 8


def draw_coverage(key, part):
    start_key, pick_key, wrap_key = jax.random.split(key, 3)
    starts = jax.random.randint(start_key, (MODULES,), 0, NTILE)
    chosen = jax.random.randint(pick_key, (), 0, MODULES)
    wrapped = NTILE - 1 - jax.random.randint(wrap_key, (), 0, TPM - 1)
    starts = jnp.where(jnp.arange(MODULES) == chosen, wrapped, starts)
    return ((starts[:, None] + jnp.arange(TPM)[None, :]) % NTILE).astype(jnp.int32)


def levels(key, extent, shards, least, top_value):
    factor_of, own = 1.0, jax.random.fold_in(key, 6)
    for dim, blocks in shards:
        draws = jnp.exp(jax.random.uniform(jax.random.fold_in(own, dim), (blocks,), jnp.float32, least / len(shards), top_value / len(shards)))
        factor_of = factor_of * jnp.repeat(draws, extent[dim] // blocks).reshape([-1 if axis == dim else 1 for axis in range(len(extent))])
    return factor_of


def bell_draw(key, dims, scale, limit, shards=(), kind=jnp.bfloat16):
    values = jax.random.normal(key, dims, jnp.float32) * scale
    if len(shards) > 0:
        values = levels(key, dims, shards, -0.22, 0.18) * values
    return jnp.clip(values, min=-limit, max=limit).astype(kind)


def setup_inputs(seed: int = 0) -> dict:
    keys = jax.random.split(jax.random.key(seed), 7)
    frames = bell_draw(keys[0], (FRAMES, MODULES * PIX), 1.0, 6.0, ((0, 4), (1, 8)))
    weights = jnp.clip(0.25 * jax.random.uniform(keys[1], (MODULES * TPM, PB, TILE), jnp.float32) ** levels(keys[1], (MODULES * TPM, PB, TILE), ((0, 8),), -0.2, 0.2), 0.0, 0.25).astype(jnp.bfloat16)
    monitor = jnp.clip(jnp.exp(math.log(2.0) - 1.3862944 * jax.random.uniform(keys[2], (FRAMES,), jnp.float32) ** levels(keys[2], (FRAMES,), ((0, 4),), -0.2, 0.2)), 0.5, 2.0)
    coverage = draw_coverage(jax.random.fold_in(keys[6], 71), 0)
    block_slot = jax.vmap(lambda own: jax.random.permutation(own, TPM))(jax.random.split(keys[4], MODULES)).reshape((MODULES, TPM)).astype(jnp.int32)
    angle_index = jax.random.randint(keys[5], (ANGLES,), 0, ASTEPS).astype(jnp.int32)
    return dict(frames=frames, weights=weights, monitor=monitor, coverage=coverage, block_slot=block_slot, angle_index=angle_index)


def ramp_table(length):
    places = jnp.arange(length, dtype=jnp.int32)
    offset = places[:, None] - places[None, :]
    is_odd = (offset % 2) != 0
    scaled = math.pi * offset.astype(jnp.float32)
    safe_den = jnp.where(is_odd, scaled, jnp.float32(1.0))
    return jnp.where(offset == 0, jnp.float32(0.25), jnp.where(is_odd, -1.0 / (safe_den * safe_den), jnp.float32(0.0)))


def spot_table(angle_index, row_count, length):
    theta_rad = angle_index.astype(jnp.float32) * (math.pi / ASTEPS)
    centre = (length - 1) / 2.0
    across = jnp.arange(length, dtype=jnp.float32) - centre
    down_pos = jnp.arange(row_count, dtype=jnp.float32) - (row_count - 1) / 2.0
    spot_grid = across[None, None, :] * jnp.cos(theta_rad)[:, None, None] + down_pos[None, :, None] * jnp.sin(theta_rad)[:, None, None] + centre
    return spot_grid.reshape(angle_index.shape[0], row_count * length)


def rounded_weight(spot_grid, node_pos):
    weight_val = jnp.maximum(0.0, 1.0 - jnp.abs(spot_grid - node_pos)).astype(jnp.bfloat16)
    weight_val = lax.optimization_barrier(weight_val)
    return weight_val.astype(jnp.float32)


def reference(frames, weights, monitor, coverage, block_slot, angle_index):
    group_count = TPM // SPLITS
    pixel_count = group_count * PB

    def add_module(summed, module_pos):
        module_frames = lax.dynamic_slice_in_dim(frames, module_pos * pixel_count, pixel_count, 1)
        module_frames = module_frames.astype(jnp.float32).reshape(FRAMES, group_count, PB)
        module_tiles = lax.dynamic_slice_in_dim(weights, module_pos * TPM, TPM, 0)
        module_tiles = module_tiles.astype(jnp.float32).reshape(group_count, SPLITS, PB, TILE)
        block_bins = jnp.einsum("fgp,gspc->fgsc", module_frames, module_tiles).reshape(FRAMES, TPM, TILE)
        tile_ids = coverage[module_pos][block_slot[module_pos]]
        return summed.at[:, tile_ids, :].add(block_bins), None

    summed, _ = lax.scan(add_module, jnp.zeros((FRAMES, NTILE, TILE), jnp.float32), jnp.arange(MODULES, dtype=jnp.int32))
    binned = (summed / monitor[:, None, None]).reshape(ANGLES, TRANS, NTILE * TILE)
    filtered = jnp.einsum("apb,pq->abq", binned, ramp_table(TRANS), precision=lax.Precision.HIGHEST).astype(jnp.bfloat16)

    spot_grid = spot_table(angle_index, ROWS, TRANS)
    lower_pos = jnp.floor(spot_grid)
    upper_pos = lower_pos + 1.0
    w_lower = rounded_weight(spot_grid, lower_pos)
    w_upper = rounded_weight(spot_grid, upper_pos)
    w_lower = jnp.where((lower_pos >= 0.0) & (lower_pos <= TRANS - 1.0), w_lower, 0.0)
    w_upper = jnp.where((upper_pos >= 0.0) & (upper_pos <= TRANS - 1.0), w_upper, 0.0)
    idx_lower = jnp.clip(lower_pos, 0.0, TRANS - 1.0).astype(jnp.int32)
    idx_upper = jnp.clip(upper_pos, 0.0, TRANS - 1.0).astype(jnp.int32)

    tile_major = filtered.reshape(ANGLES, NTILE, TILE, TRANS).transpose(1, 0, 2, 3)

    def one_tile(values):
        values = values.astype(jnp.float32)
        low_pick = jnp.take_along_axis(values, jnp.broadcast_to(idx_lower[:, None, :], (ANGLES, TILE, ROWS * TRANS)), axis=2)
        high_pick = jnp.take_along_axis(values, jnp.broadcast_to(idx_upper[:, None, :], (ANGLES, TILE, ROWS * TRANS)), axis=2)
        return jnp.sum(low_pick * w_lower[:, None, :] + high_pick * w_upper[:, None, :], axis=0)

    slices = lax.map(one_tile, tile_major)
    slices = (slices * (math.pi / ANGLES)).astype(jnp.bfloat16)
    return slices.reshape(QT, GROUPS, MODULES, TILE, ROWS * TRANS)
```

```python
import functools
import math

import jax
import jax.numpy as jnp
from jax import lax
from jax.experimental import pallas as pl
from jax.experimental.pallas import tpu as pltpu
from jax.sharding import PartitionSpec as P

TRANS = 512
ASTEPS = 180
ROWS = 16
NTILE = 256
MIB = 1024 * 1024


def ramp_table(length):
    places = jnp.arange(length, dtype=jnp.int32)
    offset = places[:, None] - places[None, :]
    is_odd = offset % 2 != 0
    scaled = math.pi * offset.astype(jnp.float32)
    safe_den = jnp.where(is_odd, scaled, jnp.float32(1.0))
    return jnp.where(
        offset == 0,
        jnp.float32(0.25),
        jnp.where(is_odd, -1.0 / (safe_den * safe_den), jnp.float32(0.0)),
    )


def spot_table(angle_index, row_count, length):
    theta_rad = angle_index.astype(jnp.float32) * (math.pi / ASTEPS)
    centre = (length - 1) / 2.0
    across = jnp.arange(length, dtype=jnp.float32) - centre
    down_pos = jnp.arange(row_count, dtype=jnp.float32) - (row_count - 1) / 2.0
    spot_grid = (
        across[None, None, :] * jnp.cos(theta_rad)[:, None, None]
        + down_pos[None, :, None] * jnp.sin(theta_rad)[:, None, None]
        + centre
    )
    return spot_grid.reshape(angle_index.shape[0], row_count * length)


def plane_of(modules):
    wide = max(w for w in range(1, modules + 1) if modules % w == 0 and w * w <= modules)
    return modules // wide, wide


def split_kernel(splits, place_ref, frames_ref, weights_ref, monitor_ref, out_ref):
    group = pl.program_id(0)
    scale = 1.0 / monitor_ref[...]
    for part in range(splits):
        bins = jnp.dot(frames_ref[...], weights_ref[part], preferred_element_type=jnp.float32)
        out_ref[place_ref[group * splits + part]] = bins * scale


def split(frames, weights, monitor, places):
    fr_dev, pixel_count = frames.shape
    slot_count, group_pixels, tile_width = weights.shape
    group_count = pixel_count // group_pixels
    splits = slot_count // group_count
    return pl.pallas_call(
        functools.partial(split_kernel, splits),
        out_shape=jax.ShapeDtypeStruct((slot_count, fr_dev, tile_width), jnp.float32),
        grid_spec=pltpu.PrefetchScalarGridSpec(
            num_scalar_prefetch=1,
            grid=(group_count,),
            in_specs=[
                pl.BlockSpec((fr_dev, group_pixels), lambda g, _: (0, g)),
                pl.BlockSpec((splits, group_pixels, tile_width), lambda g, _: (g, 0, 0)),
                pl.BlockSpec((fr_dev, 1), lambda g, _: (0, 0)),
            ],
            out_specs=pl.BlockSpec((slot_count, fr_dev, tile_width), lambda g, _: (0, 0, 0)),
        ),
        compiler_params=pltpu.CompilerParams(vmem_limit_bytes=48 * MIB),
        cost_estimate=pl.CostEstimate(
            flops=2 * fr_dev * slot_count * group_pixels * tile_width,
            bytes_accessed=frames.size * 2 + weights.size * 2 + slot_count * fr_dev * tile_width * 4,
            transcendentals=0,
        ),
    )(places, frames, weights, monitor[:, None])


def exchange_kernel(
    plan, rank_ref, bins_ref, out_ref,
    merge_in, owner_in, dense_out, dense_in, owned, merge_work, owner_work,
    merge_send, merge_recv, owner_send, owner_recv, dense_send, dense_recv,
    frame_send, frame_recv, local_sem,
):
    groups, modules, deep, wide, chunks, rows, per_peer, local_tiles = plan
    deep_half = deep // 2
    sources = deep_half * wide
    fr_dev = chunks * rows
    frame_pos = lax.axis_index("frame")
    module_pos = lax.axis_index("module")
    z_pos, x_pos = module_pos // wide, module_pos % wide
    half = z_pos // deep_half
    first_z, other_z = half * deep_half, (1 - half) * deep_half
    place = (z_pos - first_z) * wide + x_pos
    merge_z = jnp.where(half == 0, deep_half - 1, deep_half)
    merges = z_pos == merge_z

    barrier = pltpu.get_barrier_semaphore()
    for step in range(1, modules):
        pl.semaphore_signal(
            barrier, inc=1, device_id=(frame_pos, lax.rem(module_pos + step, modules)),
            device_id_type=pl.DeviceIdType.MESH,
        )
    for step in range(1, groups):
        pl.semaphore_signal(
            barrier, inc=1, device_id=(lax.rem(frame_pos + step, groups), module_pos),
            device_id_type=pl.DeviceIdType.MESH,
        )
    pl.semaphore_wait(barrier, modules + groups - 2)

    def chunk_of(c):
        return pl.ds(pl.multiple_of(c * rows, rows), rows)

    def remote(src, dst, send, recv, frame, module):
        return pltpu.make_async_remote_copy(
            src_ref=src, dst_ref=dst, send_sem=send, recv_sem=recv,
            device_id=(frame, module), device_id_type=pl.DeviceIdType.MESH,
        )

    def merge_copy(c, target_x, source):
        return remote(
            bins_ref.at[target_x, pl.ds(other_z, deep_half), :, chunk_of(c), :],
            merge_in.at[source, :, :, chunk_of(c), :],
            merge_send.at[target_x, c], merge_recv.at[source, c],
            frame_pos, merge_z * wide + target_x,
        )

    def owner_copy(c, target, source):
        target_z, target_x = first_z + target // wide, target % wide
        return remote(
            bins_ref.at[target_x, target_z, :, chunk_of(c), :],
            owner_in.at[source, :, chunk_of(c), :],
            owner_send.at[target, c], owner_recv.at[source, c],
            frame_pos, target_z * wide + target_x,
        )

    def dense_copy(c, i):
        return remote(
            dense_out.at[i, :, chunk_of(c), :], dense_in.at[:, chunk_of(c), :],
            dense_send.at[i, c], dense_recv.at[c],
            frame_pos, (other_z + i) * wide + x_pos,
        )

    def frame_copy(c, target, source):
        start = pl.multiple_of(source * fr_dev + c * rows, rows)
        return remote(
            owned.at[target, :, chunk_of(c), :], out_ref.at[:, pl.ds(start, rows), :],
            frame_send.at[target, c], frame_recv.at[source, c],
            target, module_pos,
        )

    def own_merge():
        return pltpu.make_async_copy(
            bins_ref.at[x_pos, pl.ds(other_z, deep_half)], merge_in.at[place], local_sem.at[0]
        )

    def own_owner():
        return pltpu.make_async_copy(
            bins_ref.at[x_pos, z_pos], owner_in.at[place], local_sem.at[1]
        )

    def own_frame(c):
        start = pl.multiple_of(frame_pos * fr_dev + c * rows, rows)
        return pltpu.make_async_copy(
            owned.at[frame_pos, :, chunk_of(c), :], out_ref.at[:, pl.ds(start, rows), :],
            frame_recv.at[frame_pos, c],
        )

    def start_merge(c):
        for target_x in range(wide):
            @pl.when(jnp.logical_not(merges & (x_pos == target_x)))
            def _():
                merge_copy(c, target_x, place).start()

    def sent_merge(c):
        for target_x in range(wide):
            @pl.when(jnp.logical_not(merges & (x_pos == target_x)))
            def _():
                merge_copy(c, target_x, place).wait_send()

    def start_owner(c):
        for target in range(sources):
            @pl.when(place != target)
            def _():
                owner_copy(c, target, place).start()

    def sent_owner(c):
        for target in range(sources):
            @pl.when(place != target)
            def _():
                owner_copy(c, target, place).wait_send()

    ahead = min(2, chunks)
    for c in range(ahead):
        start_merge(c)

    @pl.when(merges)
    def _():
        own_merge().start()

    own_owner().start()

    @pl.when(merges)
    def _():
        own_merge().wait()

    def pick(buffer_at, row):
        rank = rank_ref[row]
        value = buffer_at(jnp.maximum(rank, 0))
        return value * (rank >= 0).astype(jnp.float32)

    def merge_step(c, _):
        @pl.when(merges)
        def _():
            for source in range(sources):
                @pl.when(place != source)
                def _():
                    merge_copy(c, 0, source).wait_recv()

            for source in range(sources):
                merge_work[source] = merge_in[source, :, :, chunk_of(c), :]

            def merge_tile(l, _):
                for i in range(deep_half):
                    total = None
                    for source in range(sources):
                        term = pick(
                            lambda r: merge_work[source, i, r],
                            (source * (deep_half + 1) + 1 + i) * local_tiles + l,
                        )
                        total = term if total is None else total + term
                    dense_out[i, l, chunk_of(c), :] = total
                return 0

            lax.fori_loop(0, local_tiles, merge_tile, 0)
            for i in range(deep_half):
                dense_copy(c, i).start()

        sent_merge(c)

        @pl.when(c + ahead < chunks)
        def _():
            start_merge(c + ahead)

        return 0

    lax.fori_loop(0, chunks, merge_step, 0)

    for c in range(ahead):
        start_owner(c)
    own_owner().wait()

    def owner_step(c, _):
        for source in range(sources):
            @pl.when(place != source)
            def _():
                owner_copy(c, 0, source).wait_recv()

        dense_copy(c, 0).wait_recv()

        for source in range(sources):
            owner_work[source] = owner_in[source, :, chunk_of(c), :]

        def owner_tile(q, _):
            for f in range(groups):
                l = q * groups + f
                total = dense_in[l, chunk_of(c), :]
                for source in range(sources):
                    total = total + pick(
                        lambda r: owner_work[source, r],
                        source * (deep_half + 1) * local_tiles + l,
                    )
                owned[f, q, chunk_of(c), :] = total
            return 0

        lax.fori_loop(0, local_tiles // groups, owner_tile, 0)
        for f in range(groups):
            @pl.when(frame_pos != f)
            def _():
                frame_copy(c, f, frame_pos).start()

        own_frame(c).start()
        sent_owner(c)

        @pl.when(c + ahead < chunks)
        def _():
            start_owner(c + ahead)

        return 0

    lax.fori_loop(0, chunks, owner_step, 0)

    def finish(c, _):
        @pl.when(merges)
        def _():
            for i in range(deep_half):
                dense_copy(c, i).wait_send()

        for f in range(groups):
            @pl.when(frame_pos != f)
            def _():
                frame_copy(c, f, frame_pos).wait_send()
                frame_copy(c, f, f).wait_recv()

        own_frame(c).wait()
        return 0

    lax.fori_loop(0, chunks, finish, 0)


def exchange(bins, ranks, groups, modules, local_tiles, chunks):
    wide, deep, per_peer, fr_dev, width = bins.shape
    deep_half = deep // 2
    sources = deep_half * wide
    rows = fr_dev // chunks
    plan = (groups, modules, deep, wide, chunks, rows, per_peer, local_tiles)
    dma = pltpu.SemaphoreType.DMA
    return pl.pallas_call(
        functools.partial(exchange_kernel, plan),
        out_shape=jax.ShapeDtypeStruct((local_tiles // groups, groups * fr_dev, width), jnp.float32),
        in_specs=[
            pl.BlockSpec(memory_space=pltpu.SMEM),
            pl.BlockSpec(memory_space=pl.ANY),
        ],
        out_specs=pl.BlockSpec(memory_space=pl.ANY),
        scratch_shapes=[
            pltpu.VMEM((sources, deep_half, per_peer, fr_dev, width), jnp.float32),
            pltpu.VMEM((sources, per_peer, fr_dev, width), jnp.float32),
            pltpu.VMEM((deep_half, local_tiles, fr_dev, width), jnp.float32),
            pltpu.VMEM((local_tiles, fr_dev, width), jnp.float32),
            pltpu.VMEM((groups, local_tiles // groups, fr_dev, width), jnp.float32),
            pltpu.VMEM((sources, deep_half, per_peer, rows, width), jnp.float32),
            pltpu.VMEM((sources, per_peer, rows, width), jnp.float32),
            dma((wide, chunks)),
            dma((sources, chunks)),
            dma((sources, chunks)),
            dma((sources, chunks)),
            dma((deep_half, chunks)),
            dma((chunks,)),
            dma((groups, chunks)),
            dma((groups, chunks)),
            dma((2,)),
        ],
        compiler_params=pltpu.CompilerParams(
            collective_id=0, has_side_effects=True, vmem_limit_bytes=48 * MIB
        ),
        cost_estimate=pl.CostEstimate(
            flops=bins.size, bytes_accessed=bins.size * 8, transcendentals=0
        ),
    )(ranks, bins)


def project_kernel(angles, items, sino_ref, ramp_ref, spot_ref, out_ref, filtered):
    length = ramp_ref.shape[0]
    width = sino_ref.shape[2]

    @pl.when(pl.program_id(0) == 0)
    def _():
        def filter_item(item, _):
            for angle in range(angles):
                lines = sino_ref[item, angle * length : (angle + 1) * length, :]
                line_rows = lax.dot_general(
                    lines.T, ramp_ref[...], (((1,), (0,)), ((), ())),
                    precision=lax.Precision.HIGHEST, preferred_element_type=jnp.float32,
                )
                filtered[
                    pl.ds(pl.multiple_of(item * width, width), width),
                    angle * length : (angle + 1) * length,
                ] = line_rows.astype(jnp.bfloat16)
            return 0

        lax.fori_loop(0, items, filter_item, 0)

    columns = out_ref.shape[2]
    positions = lax.broadcasted_iota(jnp.int32, (length, columns), 0).astype(jnp.float32)
    total = None
    for angle in range(angles):
        table = jnp.maximum(
            0.0, 1.0 - jnp.abs(spot_ref[angle : angle + 1, :] - positions)
        ).astype(jnp.bfloat16)
        part = jnp.dot(
            filtered[:, angle * length : (angle + 1) * length], table,
            preferred_element_type=jnp.float32,
        )
        total = part if total is None else total + part
    out_ref[...] = (total * (math.pi / angles)).astype(jnp.bfloat16).reshape(out_ref.shape)


def project(sinogram, ramp_filter, spot_grid):
    items, frame_count, width = sinogram.shape
    angles, column_count = spot_grid.shape
    length = ramp_filter.shape[0]
    block = length
    return pl.pallas_call(
        functools.partial(project_kernel, angles, items),
        out_shape=jax.ShapeDtypeStruct((items, width, column_count), jnp.bfloat16),
        grid=(column_count // block,),
        in_specs=[
            pl.BlockSpec((items, frame_count, width), lambda j: (0, 0, 0)),
            pl.BlockSpec((length, length), lambda j: (0, 0)),
            pl.BlockSpec((angles, block), lambda j: (0, j)),
        ],
        out_specs=pl.BlockSpec((items, width, block), lambda j: (0, 0, j)),
        scratch_shapes=[pltpu.VMEM((items * width, frame_count), jnp.bfloat16)],
        compiler_params=pltpu.CompilerParams(vmem_limit_bytes=48 * MIB),
        cost_estimate=pl.CostEstimate(
            flops=2 * items * width * frame_count * column_count,
            bytes_accessed=sinogram.size * 4 + items * width * column_count * 2,
            transcendentals=0,
        ),
    )(sinogram, ramp_filter, spot_grid)


def on_device(frames, weights, monitor, coverage, block_slot, angle_index):
    groups = lax.axis_size("frame")
    modules = lax.axis_size("module")
    module_pos = lax.axis_index("module")
    deep, wide = plane_of(modules)
    fr_dev = frames.shape[0]
    slot_count, _, tile_width = weights.shape
    local_tiles = NTILE // modules
    per_peer = slot_count // modules
    starts = coverage[:, 0]

    own_slots = block_slot[0]
    owner = (starts[module_pos] + own_slots) % modules
    places = ((owner % wide) * deep + owner // wide) * per_peer + own_slots // modules
    bins = split(frames, weights, monitor, places)
    bins = bins.reshape(wide, deep, per_peer, fr_dev, tile_width)

    deep_half = deep // 2
    z_pos, x_pos = module_pos // wide, module_pos % wide
    half = z_pos // deep_half
    source_module = half * deep_half * wide + jnp.arange(deep_half * wide, dtype=jnp.int32)
    target_module = jnp.concatenate([
        module_pos[None],
        ((1 - half) * deep_half + jnp.arange(deep_half, dtype=jnp.int32)) * wide + x_pos,
    ])
    tiles = (
        jnp.arange(local_tiles, dtype=jnp.int32)[None, None, :] * modules
        + target_module[None, :, None]
    )
    slots = (tiles - starts[source_module][:, None, None]) % NTILE
    ranks = jnp.where(slots < slot_count, slots // modules, -1).reshape(-1)
    sinogram = exchange(bins, ranks, groups, modules, local_tiles, 8)

    slices = project(sinogram, ramp_table(TRANS), spot_table(angle_index, ROWS, TRANS))
    return slices.reshape(slices.shape[0], 1, 1, tile_width, ROWS * TRANS)


def solution(mesh):
    placed = (
        P("frame", "module"),
        P("module", None, None),
        P("frame"),
        P(),
        P("module", None),
        P(),
    )
    return jax.shard_map(
        on_device,
        mesh=mesh,
        in_specs=placed,
        out_specs=P(None, "frame", "module", None, None),
        check_vma=False,
    )
```

```python
import functools
import math

import jax
import jax.numpy as jnp
from jax import lax
from jax.experimental import pallas as pl
from jax.experimental.pallas import tpu as pltpu
from jax.sharding import PartitionSpec as P

TRANS = 512
ASTEPS = 180
ROWS = 16
NTILE = 256
MIB = 1024 * 1024


def ramp_table(length):
    places = jnp.arange(length, dtype=jnp.int32)
    offset = places[:, None] - places[None, :]
    is_odd = offset % 2 != 0
    scaled = math.pi * offset.astype(jnp.float32)
    safe_den = jnp.where(is_odd, scaled, jnp.float32(1.0))
    return jnp.where(
        offset == 0,
        jnp.float32(0.25),
        jnp.where(is_odd, -1.0 / (safe_den * safe_den), jnp.float32(0.0)),
    )


def spot_table(angle_index, row_count, length):
    theta_rad = angle_index.astype(jnp.float32) * (math.pi / ASTEPS)
    centre = (length - 1) / 2.0
    across = jnp.arange(length, dtype=jnp.float32) - centre
    down_pos = jnp.arange(row_count, dtype=jnp.float32) - (row_count - 1) / 2.0
    spot_grid = (
        across[None, None, :] * jnp.cos(theta_rad)[:, None, None]
        + down_pos[None, :, None] * jnp.sin(theta_rad)[:, None, None]
        + centre
    )
    return spot_grid.reshape(angle_index.shape[0], row_count * length)


def plane_of(modules):
    wide = max(w for w in range(1, modules + 1) if modules % w == 0 and w * w <= modules)
    return modules // wide, wide


def split_kernel(splits, place_ref, frames_ref, weights_ref, monitor_ref, out_ref):
    group = pl.program_id(0)
    scale = 1.0 / monitor_ref[...]
    tile_width = weights_ref.shape[2]
    joined = jnp.concatenate([weights_ref[part] for part in range(splits)], axis=1)
    bins = jnp.dot(frames_ref[...], joined, preferred_element_type=jnp.float32)
    for part in range(splits):
        out_ref[place_ref[group * splits + part]] = (
            bins[:, part * tile_width : (part + 1) * tile_width] * scale
        )


def split(frames, weights, monitor, places):
    fr_dev, pixel_count = frames.shape
    slot_count, group_pixels, tile_width = weights.shape
    group_count = pixel_count // group_pixels
    splits = slot_count // group_count
    return pl.pallas_call(
        functools.partial(split_kernel, splits),
        out_shape=jax.ShapeDtypeStruct((slot_count, fr_dev, tile_width), jnp.float32),
        grid_spec=pltpu.PrefetchScalarGridSpec(
            num_scalar_prefetch=1,
            grid=(group_count,),
            in_specs=[
                pl.BlockSpec((fr_dev, group_pixels), lambda g, _: (0, g)),
                pl.BlockSpec((splits, group_pixels, tile_width), lambda g, _: (g, 0, 0)),
                pl.BlockSpec((fr_dev, 1), lambda g, _: (0, 0)),
            ],
            out_specs=pl.BlockSpec((slot_count, fr_dev, tile_width), lambda g, _: (0, 0, 0)),
        ),
        compiler_params=pltpu.CompilerParams(vmem_limit_bytes=48 * MIB),
        cost_estimate=pl.CostEstimate(
            flops=2 * fr_dev * slot_count * group_pixels * tile_width,
            bytes_accessed=frames.size * 2 + weights.size * 2 + slot_count * fr_dev * tile_width * 4,
            transcendentals=0,
        ),
    )(places, frames, weights, monitor[:, None])


def exchange_kernel(
    plan, rank_ref, bins_ref, out_ref,
    merge_in, owner_in, dense_out, dense_in, owned, merge_work, owner_work,
    merge_send, merge_recv, owner_send, owner_recv, dense_send, dense_recv,
    frame_send, frame_recv, local_sem,
):
    groups, modules, deep, wide, chunks, rows, per_peer, local_tiles = plan
    deep_half = deep // 2
    sources = deep_half * wide
    fr_dev = chunks * rows
    frame_pos = lax.axis_index("frame")
    module_pos = lax.axis_index("module")
    z_pos, x_pos = module_pos // wide, module_pos % wide
    half = z_pos // deep_half
    first_z, other_z = half * deep_half, (1 - half) * deep_half
    place = (z_pos - first_z) * wide + x_pos
    merge_z = jnp.where(half == 0, deep_half - 1, deep_half)
    merges = z_pos == merge_z

    barrier = pltpu.get_barrier_semaphore()
    for step in range(1, modules):
        pl.semaphore_signal(
            barrier, inc=1, device_id=(frame_pos, lax.rem(module_pos + step, modules)),
            device_id_type=pl.DeviceIdType.MESH,
        )
    for step in range(1, groups):
        pl.semaphore_signal(
            barrier, inc=1, device_id=(lax.rem(frame_pos + step, groups), module_pos),
            device_id_type=pl.DeviceIdType.MESH,
        )
    pl.semaphore_wait(barrier, modules + groups - 2)

    def chunk_of(c):
        return pl.ds(pl.multiple_of(c * rows, rows), rows)

    def remote(src, dst, send, recv, frame, module):
        return pltpu.make_async_remote_copy(
            src_ref=src, dst_ref=dst, send_sem=send, recv_sem=recv,
            device_id=(frame, module), device_id_type=pl.DeviceIdType.MESH,
        )

    def merge_copy(c, target_x, source):
        return remote(
            bins_ref.at[target_x, pl.ds(other_z, deep_half), :, chunk_of(c), :],
            merge_in.at[source, :, :, chunk_of(c), :],
            merge_send.at[target_x, c], merge_recv.at[source, c],
            frame_pos, merge_z * wide + target_x,
        )

    def owner_copy(c, target, source):
        target_z, target_x = first_z + target // wide, target % wide
        return remote(
            bins_ref.at[target_x, target_z, :, chunk_of(c), :],
            owner_in.at[source, :, chunk_of(c), :],
            owner_send.at[target, c], owner_recv.at[source, c],
            frame_pos, target_z * wide + target_x,
        )

    def dense_copy(c, i):
        return remote(
            dense_out.at[i, :, chunk_of(c), :], dense_in.at[:, chunk_of(c), :],
            dense_send.at[i, c], dense_recv.at[c],
            frame_pos, (other_z + i) * wide + x_pos,
        )

    def frame_copy(c, target, source):
        start = pl.multiple_of(source * fr_dev + c * rows, rows)
        return remote(
            owned.at[target, :, chunk_of(c), :], out_ref.at[:, pl.ds(start, rows), :],
            frame_send.at[target, c], frame_recv.at[source, c],
            target, module_pos,
        )

    def own_merge():
        return pltpu.make_async_copy(
            bins_ref.at[x_pos, pl.ds(other_z, deep_half)], merge_in.at[place], local_sem.at[0]
        )

    def own_owner():
        return pltpu.make_async_copy(
            bins_ref.at[x_pos, z_pos], owner_in.at[place], local_sem.at[1]
        )

    def own_frame(c):
        start = pl.multiple_of(frame_pos * fr_dev + c * rows, rows)
        return pltpu.make_async_copy(
            owned.at[frame_pos, :, chunk_of(c), :], out_ref.at[:, pl.ds(start, rows), :],
            frame_recv.at[frame_pos, c],
        )

    def start_merge(c):
        for target_x in range(wide):
            @pl.when(jnp.logical_not(merges & (x_pos == target_x)))
            def _():
                merge_copy(c, target_x, place).start()

    def sent_merge(c):
        for target_x in range(wide):
            @pl.when(jnp.logical_not(merges & (x_pos == target_x)))
            def _():
                merge_copy(c, target_x, place).wait_send()

    def start_owner(c):
        for target in range(sources):
            @pl.when(place != target)
            def _():
                owner_copy(c, target, place).start()

    def sent_owner(c):
        for target in range(sources):
            @pl.when(place != target)
            def _():
                owner_copy(c, target, place).wait_send()

    ahead = min(2, chunks)
    for c in range(ahead):
        start_merge(c)

    @pl.when(merges)
    def _():
        own_merge().start()

    own_owner().start()

    @pl.when(merges)
    def _():
        own_merge().wait()

    def pick(buffer_at, row):
        rank = rank_ref[row]
        value = buffer_at(jnp.maximum(rank, 0))
        return value * (rank >= 0).astype(jnp.float32)

    def merge_step(c, _):
        @pl.when(merges)
        def _():
            start_owner(c)
            for source in range(sources):
                @pl.when(place != source)
                def _():
                    merge_copy(c, 0, source).wait_recv()

            for source in range(sources):
                merge_work[source] = merge_in[source, :, :, chunk_of(c), :]

            def merge_tile(l, _):
                for i in range(deep_half):
                    total = None
                    for source in range(sources):
                        term = pick(
                            lambda r: merge_work[source, i, r],
                            (source * (deep_half + 1) + 1 + i) * local_tiles + l,
                        )
                        total = term if total is None else total + term
                    dense_out[i, l, chunk_of(c), :] = total
                return 0

            lax.fori_loop(0, local_tiles, merge_tile, 0)
            for i in range(deep_half):
                dense_copy(c, i).start()

        sent_merge(c)

        @pl.when(c + ahead < chunks)
        def _():
            start_merge(c + ahead)

        return 0

    lax.fori_loop(0, chunks, merge_step, 0)

    @pl.when(jnp.logical_not(merges))
    def _():
        for c in range(ahead):
            start_owner(c)

    own_owner().wait()

    def owner_step(c, _):
        for source in range(sources):
            @pl.when(place != source)
            def _():
                owner_copy(c, 0, source).wait_recv()

        dense_copy(c, 0).wait_recv()

        for source in range(sources):
            owner_work[source] = owner_in[source, :, chunk_of(c), :]

        def owner_tile(q, _):
            for f in range(groups):
                l = q * groups + f
                total = dense_in[l, chunk_of(c), :]
                for source in range(sources):
                    total = total + pick(
                        lambda r: owner_work[source, r],
                        source * (deep_half + 1) * local_tiles + l,
                    )
                owned[f, q, chunk_of(c), :] = total
            return 0

        lax.fori_loop(0, local_tiles // groups, owner_tile, 0)
        for f in range(groups):
            @pl.when(frame_pos != f)
            def _():
                frame_copy(c, f, frame_pos).start()

        own_frame(c).start()
        sent_owner(c)

        @pl.when(jnp.logical_not(merges) & (c + ahead < chunks))
        def _():
            start_owner(c + ahead)

        return 0

    lax.fori_loop(0, chunks, owner_step, 0)

    def finish(c, _):
        @pl.when(merges)
        def _():
            for i in range(deep_half):
                dense_copy(c, i).wait_send()

        for f in range(groups):
            @pl.when(frame_pos != f)
            def _():
                frame_copy(c, f, frame_pos).wait_send()
                frame_copy(c, f, f).wait_recv()

        own_frame(c).wait()
        return 0

    lax.fori_loop(0, chunks, finish, 0)


def exchange(bins, ranks, groups, modules, local_tiles, chunks):
    wide, deep, per_peer, fr_dev, width = bins.shape
    deep_half = deep // 2
    sources = deep_half * wide
    rows = fr_dev // chunks
    plan = (groups, modules, deep, wide, chunks, rows, per_peer, local_tiles)
    dma = pltpu.SemaphoreType.DMA
    return pl.pallas_call(
        functools.partial(exchange_kernel, plan),
        out_shape=jax.ShapeDtypeStruct((local_tiles // groups, groups * fr_dev, width), jnp.float32),
        in_specs=[
            pl.BlockSpec(memory_space=pltpu.SMEM),
            pl.BlockSpec(memory_space=pl.ANY),
        ],
        out_specs=pl.BlockSpec(memory_space=pl.ANY),
        scratch_shapes=[
            pltpu.VMEM((sources, deep_half, per_peer, fr_dev, width), jnp.float32),
            pltpu.VMEM((sources, per_peer, fr_dev, width), jnp.float32),
            pltpu.VMEM((deep_half, local_tiles, fr_dev, width), jnp.float32),
            pltpu.VMEM((local_tiles, fr_dev, width), jnp.float32),
            pltpu.VMEM((groups, local_tiles // groups, fr_dev, width), jnp.float32),
            pltpu.VMEM((sources, deep_half, per_peer, rows, width), jnp.float32),
            pltpu.VMEM((sources, per_peer, rows, width), jnp.float32),
            dma((wide, chunks)),
            dma((sources, chunks)),
            dma((sources, chunks)),
            dma((sources, chunks)),
            dma((deep_half, chunks)),
            dma((chunks,)),
            dma((groups, chunks)),
            dma((groups, chunks)),
            dma((2,)),
        ],
        compiler_params=pltpu.CompilerParams(
            collective_id=0, has_side_effects=True, vmem_limit_bytes=48 * MIB
        ),
        cost_estimate=pl.CostEstimate(
            flops=bins.size, bytes_accessed=bins.size * 8, transcendentals=0
        ),
    )(ranks, bins)


def project_kernel(angles, items, sino_ref, ramp_ref, spot_ref, out_ref, filtered, high, low):
    length = ramp_ref.shape[0]
    width = sino_ref.shape[2]

    @pl.when(pl.program_id(0) == 0)
    def _():
        ramp_high = ramp_ref[...].astype(jnp.bfloat16)
        ramp_low = (ramp_ref[...] - ramp_high.astype(jnp.float32)).astype(jnp.bfloat16)

        def turn_item(item, _):
            rows = pl.ds(pl.multiple_of(item * width, width), width)
            turned = sino_ref[item].T
            turned_high = turned.astype(jnp.bfloat16)
            high[rows, :] = turned_high
            low[rows, :] = (turned - turned_high.astype(jnp.float32)).astype(jnp.bfloat16)
            return 0

        lax.fori_loop(0, items, turn_item, 0)
        for angle in range(angles):
            lines = slice(angle * length, (angle + 1) * length)
            total = jnp.dot(high[:, lines], ramp_high, preferred_element_type=jnp.float32)
            total += jnp.dot(high[:, lines], ramp_low, preferred_element_type=jnp.float32)
            total += jnp.dot(low[:, lines], ramp_high, preferred_element_type=jnp.float32)
            filtered[:, lines] = total.astype(jnp.bfloat16)

    columns = out_ref.shape[2]
    positions = lax.broadcasted_iota(jnp.int32, (length, columns), 0).astype(jnp.float32)
    total = None
    for angle in range(angles):
        table = jnp.maximum(
            0.0, 1.0 - jnp.abs(spot_ref[angle : angle + 1, :] - positions)
        ).astype(jnp.bfloat16)
        part = jnp.dot(
            filtered[:, angle * length : (angle + 1) * length], table,
            preferred_element_type=jnp.float32,
        )
        total = part if total is None else total + part
    out_ref[...] = (total * (math.pi / angles)).astype(jnp.bfloat16).reshape(out_ref.shape)


def project(sinogram, ramp_filter, spot_grid):
    items, frame_count, width = sinogram.shape
    angles, column_count = spot_grid.shape
    length = ramp_filter.shape[0]
    block = length
    return pl.pallas_call(
        functools.partial(project_kernel, angles, items),
        out_shape=jax.ShapeDtypeStruct((items, width, column_count), jnp.bfloat16),
        grid=(column_count // block,),
        in_specs=[
            pl.BlockSpec((items, frame_count, width), lambda j: (0, 0, 0)),
            pl.BlockSpec((length, length), lambda j: (0, 0)),
            pl.BlockSpec((angles, block), lambda j: (0, j)),
        ],
        out_specs=pl.BlockSpec((items, width, block), lambda j: (0, 0, j)),
        scratch_shapes=[pltpu.VMEM((items * width, frame_count), jnp.bfloat16)] * 3,
        compiler_params=pltpu.CompilerParams(vmem_limit_bytes=48 * MIB),
        cost_estimate=pl.CostEstimate(
            flops=2 * items * width * frame_count * column_count,
            bytes_accessed=sinogram.size * 4 + items * width * column_count * 2,
            transcendentals=0,
        ),
    )(sinogram, ramp_filter, spot_grid)


def on_device(frames, weights, monitor, coverage, block_slot, angle_index):
    groups = lax.axis_size("frame")
    modules = lax.axis_size("module")
    module_pos = lax.axis_index("module")
    deep, wide = plane_of(modules)
    fr_dev = frames.shape[0]
    slot_count, _, tile_width = weights.shape
    local_tiles = NTILE // modules
    per_peer = slot_count // modules
    starts = coverage[:, 0]

    own_slots = block_slot[0]
    owner = (starts[module_pos] + own_slots) % modules
    places = ((owner % wide) * deep + owner // wide) * per_peer + own_slots // modules
    bins = split(frames, weights, monitor, places)
    bins = bins.reshape(wide, deep, per_peer, fr_dev, tile_width)

    deep_half = deep // 2
    z_pos, x_pos = module_pos // wide, module_pos % wide
    half = z_pos // deep_half
    source_module = half * deep_half * wide + jnp.arange(deep_half * wide, dtype=jnp.int32)
    target_module = jnp.concatenate([
        module_pos[None],
        ((1 - half) * deep_half + jnp.arange(deep_half, dtype=jnp.int32)) * wide + x_pos,
    ])
    tiles = (
        jnp.arange(local_tiles, dtype=jnp.int32)[None, None, :] * modules
        + target_module[None, :, None]
    )
    slots = (tiles - starts[source_module][:, None, None]) % NTILE
    ranks = jnp.where(slots < slot_count, slots // modules, -1).reshape(-1)
    sinogram = exchange(bins, ranks, groups, modules, local_tiles, 8)

    slices = project(sinogram, ramp_table(TRANS), spot_table(angle_index, ROWS, TRANS))
    return slices.reshape(slices.shape[0], 1, 1, tile_width, ROWS * TRANS)


def solution(mesh):
    placed = (
        P("frame", "module"),
        P("module", None, None),
        P("frame"),
        P(),
        P("module", None),
        P(),
    )
    return jax.shard_map(
        on_device,
        mesh=mesh,
        in_specs=placed,
        out_specs=P(None, "frame", "module", None, None),
        check_vma=False,
    )
```
